512 devices in a mesh: tensor: 8 (over z), expert: 64 (over y, x, core).
Axes of the slice: x: 4, y: 8, z: 8, core: 2. Of those that a mesh axis runs over, the one named last changes fastest.
Arguments:
- out_grad: bfloat16 [64, 32, 4096], P('expert', 'tensor'), may hold values from -6 to 6
- norm_input: bfloat16 [64, 32, 4096], P('expert', 'tensor'), may hold values from -24 to 24
- norm_gain: float32 [4096], replicated, may hold values from 0.3 to 3
- routes: int32 [64, 32, 8], P('expert'), may hold values from 0 to 63, all different within a row; in each aligned block of 32 rows (0 to 31, 32 to 63, ..., all dimensions but the last counted through in order) at most 8 rows name the same one
- route_weight: float32 [64, 32, 8], P('expert'), may hold values from 0.05 to 0.25
- gate_saved: bfloat16 [64, 512, 1024], P('expert', None, 'tensor'), may hold values from -8 to 8
- up_saved: bfloat16 [64, 512, 1024], P('expert', None, 'tensor'), may hold values from -6 to 6
- w_gate: bfloat16 [64, 4096, 1024], P('expert', None, 'tensor'), may hold values from -0.09375 to 0.09375
- w_up: bfloat16 [64, 4096, 1024], P('expert', None, 'tensor'), may hold values from -0.09375 to 0.09375
- w_down: bfloat16 [64, 1024, 4096], P('expert', 'tensor'), may hold values from -0.1875 to 0.1875
- out_proj: bfloat16 [4096, 4096], P('tensor', 'expert'), may hold values from -0.09375 to 0.09375
Outputs:
- resid_grad: bfloat16 [64, 32, 4096], P('expert', 'tensor')
- attn_grad: bfloat16 [64, 32, 4096], P('expert', None, 'tensor')
- down_grad: bfloat16 [64, 1024, 4096], P('expert', 'tensor')
The draws below stay inside these ranges and needn't reach their ends.
Inputs may be any that keep to these rules, and one draw needn't show every extreme that they name: Each token names 8 different experts. Among the tokens of one group no expert is named by more than 8 routes, and in some group some expert is named by exactly 8.
All inputs are finite; a program needn't handle non-finite values.
Results may differ from the reference program's by a relative error of at most 0.015.
Values may be sent and summed in bfloat16 or wider, within the bound.
No kernel may reach another device: no remote copies, remote signals or barrier semaphores. Data moves between devices by JAX's collectives and lax.ppermute only.
A program may use at most 64 MiB of HBM per device.

```python
import math
import jax
import jax.numpy as jnp
import numpy as np
from jax import lax

D = 4096
HID = 1024
QDIM = 4096
TOP = 8
TOK_GRP = 32
EXPERTS = 64
GROUPS = 64
CAP = 8
SLOTS = 512
N_TENSOR = 8


def draw_norm_input(key, part):
    key_base, key_rows, key_cols = jax.random.split(key, 3)
    values = jax.random.normal(key_base, (GROUPS, TOK_GRP, D), jnp.float32)
    row_low = math.log(0.3)
    row_high = math.log(3.0)
    row_scale = jnp.exp(jax.random.uniform(key_rows, (GROUPS, TOK_GRP, 1), jnp.float32, row_low, row_high))
    col_scale = jnp.exp(jax.random.uniform(key_cols, (1, 1, D), jnp.float32, math.log(0.3), math.log(3.0)))
    return jnp.clip(values * row_scale * col_scale, -24.0, 24.0).astype(jnp.bfloat16)


def block_scale(key, dims, pieces, smallest, high):
    factor_of, own = 1.0, jax.random.fold_in(key, 6)
    for axis_at, shards_of in pieces:
        steps = jnp.exp(jax.random.uniform(jax.random.fold_in(own, axis_at), (shards_of,), jnp.float32, smallest / len(pieces), high / len(pieces)))
        factor_of = factor_of * jnp.repeat(steps, dims[axis_at] // shards_of).reshape([-1 if axis == axis_at else 1 for axis in range(len(dims))])
    return factor_of


def assign_block(rng, own, number, rows, number_of, top, bound, slope):
    ranking = jax.random.permutation(rng, number_of)
    crowded, usual = load_shares(number_of, rows * top, bound, slope, True), load_shares(number_of, rows * top, bound, slope, False)
    places = jnp.arange(number_of)

    def named(sizes, offset_by):
        used = int((sizes > 0).sum())
        fixed = max(1, used // 4)
        shifted = fixed + (places - fixed + offset_by * (used - fixed)) % max(1, number_of - fixed)
        return jnp.zeros((number_of,), jnp.int32).at[ranking[jnp.where(places < fixed, places, shifted)]].set(jnp.asarray(sizes, jnp.int32))

    sizes = jnp.where(number % 4 == 0, named(crowded, number // 4), named(usual, number - number // 4 - 1))
    mixed = jax.random.permutation(jax.random.fold_in(own, 3), number_of)
    source_of, sink = mixed[0:number_of // 2 * 2:2], mixed[1:number_of // 2 * 2:2]
    margin = jnp.minimum(sizes[source_of] - 1, bound - sizes[sink]) // 2
    margin = jnp.where((source_of == ranking[0]) | (sink == ranking[0]) | (sizes[sink] == 0), 0, jnp.maximum(margin, 0))
    shifted = jax.random.randint(jax.random.fold_in(own, 4), (number_of // 2,), 0, 1 << 20) % (margin + 1)
    sizes = sizes.at[source_of].add(-shifted).at[sink].add(shifted)
    members = jnp.searchsorted(jnp.cumsum(sizes), jnp.arange(rows * top), side="right").astype(jnp.int32)
    grid = members.reshape(top, rows).T
    grid = grid[jax.random.permutation(jax.random.fold_in(own, 1), rows)]
    offset_by = jax.random.randint(jax.random.fold_in(own, 2), (rows, 1), 0, top)
    return jnp.take_along_axis(grid, (jnp.arange(top)[None, :] + offset_by) % top, axis=1)


def load_shares(number_of, total, bound, skew, full):
    portions = [(1 << 20) // math.isqrt(standing ** skew) + 1 for standing in range(1, number_of + 1)]
    largest = bound if full else min(bound, max(-(-total // number_of), total * portions[0] // sum(portions)))
    least = 1 if total - largest >= number_of - 1 else 0
    holding, rest = [largest] + [least] * (number_of - 1), total - largest - least * (number_of - 1)
    while rest > 0:
        candidates = [i for i in range(1, number_of) if holding[i] < largest] or [i for i in range(1, number_of) if holding[i] < bound]
        mass, budget = sum([portions[i] for i in candidates]), rest
        for i in candidates:
            extra = min(bound - holding[i], max(1, budget * portions[i] // mass), rest)
            holding[i] = holding[i] + extra
            rest = rest - extra
    return np.array(holding)


def gaussian(key, shape, scale, most, cuts=(), held_as=jnp.bfloat16):
    factor_of = block_scale(key, shape, cuts, -0.22, 0.18) if cuts else 1.0
    drawn = jax.random.normal(key, shape, jnp.float32) * scale * factor_of
    return jnp.minimum(jnp.maximum(drawn, -most), most).astype(held_as)


def setup_inputs(seed: int = 0) -> dict:
    arg_keys = jax.random.split(jax.random.key(seed), 12)
    out_grad = gaussian(arg_keys[0], (GROUPS, TOK_GRP, D), 1.0, 6.0, ((0, 64), (1, 8)))
    norm_input = draw_norm_input(jax.random.fold_in(arg_keys[11], 71), 0)
    norm_gain = jnp.clip(jnp.exp(jax.random.uniform(arg_keys[2], (D,), jnp.float32, math.log(0.3), math.log(3.0))), 0.3, 3.0)
    routes_keys = jax.random.split(jax.random.fold_in(arg_keys[3], 1), GROUPS * TOK_GRP // TOK_GRP)
    routes_turns = jax.random.permutation(jax.random.fold_in(arg_keys[3], 3), GROUPS * TOK_GRP // TOK_GRP)
    routes = jax.vmap(lambda own, number: assign_block(jax.random.fold_in(arg_keys[3], 2), own, number, TOK_GRP, EXPERTS, TOP, CAP, 2))(routes_keys, routes_turns).reshape((GROUPS, TOK_GRP, TOP))
    route_weight = jnp.clip(0.05 + 0.2 * jax.random.uniform(arg_keys[4], (GROUPS, TOK_GRP, TOP), jnp.float32) ** block_scale(arg_keys[4], (GROUPS, TOK_GRP, TOP), ((0, 64),), -0.2, 0.2), 0.05, 0.25)
    gate_saved = gaussian(arg_keys[5], (EXPERTS, SLOTS, HID), 1.5, 8.0, ((0, 64), (2, 8)))
    up_saved = gaussian(arg_keys[6], (EXPERTS, SLOTS, HID), 1.0, 6.0, ((0, 64), (2, 8)))
    w_gate = gaussian(arg_keys[7], (EXPERTS, D, HID), D ** -0.5, 0.09375, ((0, 64), (2, 8)))
    w_up = gaussian(arg_keys[8], (EXPERTS, D, HID), D ** -0.5, 0.09375, ((0, 64), (2, 8)))
    w_down = gaussian(arg_keys[9], (EXPERTS, HID, D), HID ** -0.5, 0.1875, ((0, 64), (1, 8)))
    out_proj = gaussian(arg_keys[10], (QDIM, D), QDIM ** -0.5, 0.09375, ((0, 8), (1, 64)))
    return {"out_grad": out_grad, "norm_input": norm_input, "norm_gain": norm_gain, "routes": routes, "route_weight": route_weight, "gate_saved": gate_saved, "up_saved": up_saved, "w_gate": w_gate, "w_up": w_up, "w_down": w_down, "out_proj": out_proj}


def slot_ranks(routes):
    route_ids = routes.reshape(GROUPS, TOK_GRP * TOP)
    one_hot = (route_ids[:, :, None] == jnp.arange(EXPERTS, dtype=jnp.int32)[None, None, :]).astype(jnp.int32)
    earlier = jnp.cumsum(one_hot, axis=1) - one_hot
    slot_rank = lax.optimization_barrier(jnp.sum(earlier * one_hot, axis=2)).astype(jnp.int32)
    return (route_ids, slot_rank)

def reference(out_grad, norm_input, norm_gain, routes, route_weight, gate_saved, up_saved, w_gate, w_up, w_down, out_proj):
    route_total = TOK_GRP * TOP
    route_ids, slot_rank = slot_ranks(routes)
    position = route_ids * CAP + slot_rank
    group_index = jnp.arange(GROUPS, dtype=jnp.int32)[:, None]
    route_index = jnp.broadcast_to(jnp.arange(route_total, dtype=jnp.int32)[None, :], (GROUPS, route_total))
    source = jnp.full((GROUPS, EXPERTS * CAP), -1, jnp.int32).at[group_index, position].set(route_index)
    filled = source >= 0
    safe_source = jnp.where(filled, source, 0).astype(jnp.int32)
    weight_flat = route_weight.reshape(GROUPS, route_total)
    slot_weight = jnp.where(filled, jnp.take_along_axis(weight_flat, safe_source, axis=1), jnp.float32(0.0))
    slot_token = (safe_source // TOP).astype(jnp.int32)
    block_width = HID // N_TENSOR

    def per_expert(expert_id):
        start = (expert_id * CAP).astype(jnp.int32)
        token_ids = lax.dynamic_slice_in_dim(slot_token, start, CAP, 1)
        weights = lax.dynamic_slice_in_dim(slot_weight, start, CAP, 1)
        picked_rows = out_grad[group_index, token_ids]
        slot_grad = (weights[:, :, None] * picked_rows.astype(jnp.float32)).astype(jnp.bfloat16)
        slot_grad = slot_grad.reshape(GROUPS * CAP, D)
        gate = gate_saved[expert_id].astype(jnp.float32)
        upper = up_saved[expert_id].astype(jnp.float32)
        hid_grad = jnp.dot(slot_grad, w_down[expert_id].T, preferred_element_type=jnp.float32)
        sigmoid_gate = jax.nn.sigmoid(gate)
        activation = gate * sigmoid_gate
        gate_grad = (hid_grad * upper * sigmoid_gate * (1.0 + gate * (1.0 - sigmoid_gate))).astype(jnp.bfloat16)
        up_grad = (hid_grad * activation).astype(jnp.bfloat16)
        hidden = (activation * upper).astype(jnp.bfloat16)
        gate_blocks = gate_grad.astype(jnp.float32).reshape(GROUPS * CAP, N_TENSOR, block_width)
        up_blocks = up_grad.astype(jnp.float32).reshape(GROUPS * CAP, N_TENSOR, block_width)
        gate_weights = w_gate[expert_id].astype(jnp.float32).reshape(D, N_TENSOR, block_width)
        up_weights = w_up[expert_id].astype(jnp.float32).reshape(D, N_TENSOR, block_width)
        part_grad = jnp.einsum('jbh,dbh->bjd', gate_blocks, gate_weights) + jnp.einsum('jbh,dbh->bjd', up_blocks, up_weights)
        part_grad = part_grad.astype(jnp.bfloat16)
        slot_sum = lax.optimization_barrier(jnp.sum(part_grad.astype(jnp.float32), axis=0))
        down_grad = jnp.dot(hidden.T, slot_grad, preferred_element_type=jnp.float32).astype(jnp.bfloat16)
        return (slot_sum, down_grad)
    slot_sums, down_grad = lax.map(per_expert, jnp.arange(EXPERTS, dtype=jnp.int32))
    picked = slot_sums[route_ids, group_index * CAP + slot_rank]
    moe_grad = lax.optimization_barrier(jnp.sum(picked.reshape(GROUPS, TOK_GRP, TOP, D), axis=2))
    resid_in = norm_input.astype(jnp.float32)
    inv_rms = lax.rsqrt(lax.optimization_barrier(jnp.mean(resid_in * resid_in, axis=-1, keepdims=True)) + 1e-06)
    scaled_grad = norm_gain * moe_grad
    projection = lax.optimization_barrier(jnp.sum(scaled_grad * resid_in, axis=-1, keepdims=True))
    resid_grad = out_grad.astype(jnp.float32) + inv_rms * scaled_grad - inv_rms * inv_rms * inv_rms / D * resid_in * projection
    resid_grad = resid_grad.astype(jnp.bfloat16)
    attn_grad = jnp.dot(resid_grad.reshape(GROUPS * TOK_GRP, D), out_proj.T, preferred_element_type=jnp.float32)
    attn_grad = attn_grad.astype(jnp.bfloat16).reshape(GROUPS, TOK_GRP, QDIM)
    return (resid_grad, attn_grad, down_grad)
```

```python
import functools

import jax
import jax.numpy as jnp
from jax import lax
from jax.experimental import pallas as pl
from jax.experimental.pallas import tpu as pltpu
from jax.sharding import PartitionSpec as P

F32 = jnp.float32
BF16 = jnp.bfloat16
LAST = (((1,), (1,)), ((), ()))
FIRST = (((0,), (0,)), ((), ()))
PLAIN = (((1,), (0,)), ((), ()))
VMEM_BYTES = 48 * 1024 * 1024
OFFSETS = (0, 1, -1, 2, -2, 3, -3, 4)


def dot(a, b, dims):
    return lax.dot_general(a, b, dims, preferred_element_type=F32)


def vmem_specs(count):
    return [pl.BlockSpec(memory_space=pltpu.VMEM)] * count


def call(kernel, out_shapes, args, flops, scratch=()):
    moved = sum(a.size * a.dtype.itemsize for a in (*args, *out_shapes))
    return pl.pallas_call(
        kernel,
        out_shape=list(out_shapes),
        in_specs=vmem_specs(len(args)),
        out_specs=vmem_specs(len(out_shapes)),
        scratch_shapes=list(scratch),
        compiler_params=pltpu.CompilerParams(vmem_limit_bytes=VMEM_BYTES),
        cost_estimate=pl.CostEstimate(flops=flops, bytes_accessed=moved, transcendentals=0),
    )(*args)


def struct(shape, dtype):
    return jax.ShapeDtypeStruct(shape, dtype)


def slice_at(offset, width):
    n = lax.axis_size("tensor")
    index = lax.rem(lax.axis_index("tensor") + (offset + n), n)
    return pl.ds(pl.multiple_of(index * width, width), width)


def hid_kernel(width, *refs):
    chunks = refs[:16]
    w_down, gate_ref, up_ref, w_gate, w_up = refs[16:21]
    gate_grad_ref, up_grad_ref, hidden_ref = refs[21:24]
    far = refs[24:26]
    rows = chunks[0].shape[0]
    for half in range(2):
        total = None
        for k, offset in enumerate(OFFSETS):
            term = dot(chunks[2 * k + half][...], w_down[:, slice_at(offset, width)], LAST)
            total = term if total is None else total + term
        here = pl.ds(half * rows, rows)
        gate = gate_ref[here, :].astype(F32)
        upper = up_ref[here, :].astype(F32)
        sig = jax.nn.sigmoid(gate)
        act = gate * sig
        gate_grad = (total * upper * sig * (1.0 + gate * (1.0 - sig))).astype(BF16)
        up_grad = (total * act).astype(BF16)
        gate_grad_ref[here, :] = gate_grad
        up_grad_ref[here, :] = up_grad
        hidden_ref[here, :] = (act * upper).astype(BF16)
        cols = slice_at(4, width)
        part = dot(gate_grad, w_gate[cols, :], LAST) + dot(up_grad, w_up[cols, :], LAST)
        far[half][...] = part.astype(BF16)


def part_kernel(width, gate_grad, up_grad, w_gate, w_up, *outs):
    rows = outs[0].shape[0]
    for k, offset in enumerate((3, -3, 2, -2, 1, -1, 0)):
        cols = slice_at(offset, width)
        for half in range(2):
            here = pl.ds(half * rows, rows)
            part = dot(gate_grad[here, :], w_gate[cols, :], LAST)
            part = part + dot(up_grad[here, :], w_up[cols, :], LAST)
            outs[2 * k + half][...] = part.astype(BF16)


def down_kernel(width, *refs):
    chunks, hidden, out = refs[:16], refs[16], refs[17]
    rows = chunks[0].shape[0]
    for k, offset in enumerate(OFFSETS):
        total = dot(hidden[pl.ds(0, rows), :], chunks[2 * k][...], FIRST)
        total = total + dot(hidden[pl.ds(rows, rows), :], chunks[2 * k + 1][...], FIRST)
        out[:, slice_at(offset, width)] = total.astype(BF16)


def tail_kernel(moe_ref, rows_ref, norm_ref, gain_ref, proj_ref, resid_ref, attn_ref, held):
    n, _, width = moe_ref.shape
    model = n * width
    norm_in = norm_ref[...].astype(F32)
    inv = lax.rsqrt(jnp.sum(norm_in * norm_in, axis=-1, keepdims=True) / model + 1e-06)
    moe = jnp.concatenate([moe_ref[j] for j in range(n)], axis=1).astype(F32)
    scaled = gain_ref[...] * moe
    along = jnp.sum(scaled * norm_in, axis=-1, keepdims=True)
    resid = rows_ref[...].astype(F32) + inv * scaled - inv * inv * inv / model * norm_in * along
    held[...] = resid
    attn_ref[...] = dot(resid.astype(BF16), proj_ref[...], LAST).astype(BF16)
    own = resid_ref.shape[0]
    index = lax.axis_index("tensor")
    pair = held[pl.ds(pl.multiple_of(index // 2 * 2 * own, 2 * own), 2 * own), :]
    resid_ref[...] = jnp.where(lax.rem(index, 2) == 0, pair[:own], pair[own:]).astype(BF16)


def shift(x, step):
    n = lax.axis_size("tensor")
    return lax.ppermute(x, "tensor", [(i, (i + step) % n) for i in range(n)])


def add(a, b):
    return (a.astype(F32) + b.astype(F32)).astype(BF16)


def per_device(
    out_grad,
    norm_input,
    norm_gain,
    routes,
    route_weight,
    gate_saved,
    up_saved,
    w_gate,
    w_up,
    w_down,
    out_proj,
):
    experts = lax.axis_size("expert")
    n = lax.axis_size("tensor")
    tokens, top = routes.shape[1:]
    slots = gate_saved.shape[1]
    cap = slots // experts
    hid = gate_saved.shape[2]
    model = out_grad.shape[2]
    width = model // n
    total = tokens * top
    half = slots // 2

    ids = routes[0].reshape(total)
    number = jnp.arange(total, dtype=jnp.int32)
    same = (ids[:, None] == ids[None, :]) & (number[None, :] < number[:, None])
    rank = jnp.sum(same.astype(jnp.int32), axis=1)
    position = ids * cap + rank
    named = position[None, :] == jnp.arange(slots, dtype=jnp.int32)[:, None]
    slot_weight = jnp.sum(
        jnp.where(named, route_weight[0].reshape(1, total), 0.0), axis=1, keepdims=True
    )
    of_token = (
        number[:, None] // top == jnp.arange(tokens, dtype=jnp.int32)[None, :]
    ).astype(BF16)
    pick = dot(named.astype(BF16), of_token, PLAIN).astype(BF16)

    own_rows = lax.all_to_all(out_grad[0], "tensor", 1, 0, tiled=True)
    scaled = (slot_weight * dot(pick, own_rows, PLAIN)).astype(BF16)
    own_slots = lax.all_to_all(
        scaled.reshape(experts, cap, width), "expert", 0, 0, tiled=True
    ).reshape(slots, width)

    both = jnp.concatenate([out_grad[0], norm_input[0]], axis=0)
    both, own_slots = lax.optimization_barrier((both, own_slots))
    held = {(0, 0): own_slots[:half], (0, 1): own_slots[half:]}
    for step in range(1, 5):
        held[step, 0] = shift(held[step - 1, 0], 1)
        held[-step, 1] = shift(held[1 - step, 1], -1)
        if step < 4:
            held[step, 1] = shift(held[step - 1, 1], 1)
            held[-step, 0] = shift(held[1 - step, 0], -1)
    chunks = []
    for offset in OFFSETS:
        for which in range(2):
            key = -offset if offset != 4 else (4 if which == 0 else -4)
            chunks.append(held[key, which])

    every = lax.all_to_all(
        jnp.broadcast_to(both[None], (n, *both.shape)), "tensor", 0, 0, tiled=True
    )
    own = out_grad.shape[1]
    all_rows = every[:, :own].reshape(tokens, model)
    all_norm = every[:, own:].reshape(tokens, model)
    proj = lax.all_gather(out_proj, "expert", axis=1, tiled=True)

    half_part = struct((half, width), BF16)
    grads = struct((slots, hid), BF16)
    gate_grad, up_grad, hidden, far_a, far_b = call(
        functools.partial(hid_kernel, width),
        (grads, grads, grads, half_part, half_part),
        (*chunks, w_down[0], gate_saved[0], up_saved[0], w_gate[0], w_up[0]),
        2 * slots * model * hid,
    )
    parts = call(
        functools.partial(part_kernel, width),
        (half_part,) * 14,
        (gate_grad, up_grad, w_gate[0], w_up[0]),
        4 * slots * model * hid,
    )
    part = {(4, 0): far_a, (-4, 1): far_b}
    for k, offset in enumerate((3, -3, 2, -2, 1, -1, 0)):
        part[offset, 0], part[offset, 1] = parts[2 * k], parts[2 * k + 1]
    moving = {
        (1, 0): (4, part[4, 0]),
        (-1, 1): (4, part[-4, 1]),
        (1, 1): (3, part[3, 1]),
        (-1, 0): (3, part[-3, 0]),
    }
    for _ in range(4):
        for (way, which), (away, value) in list(moving.items()):
            if away == 0:
                continue
            value = shift(value, way)
            away -= 1
            if away:
                value = add(value, part[way * away, which])
            moving[way, which] = (away, value)
    sums = []
    for which in range(2):
        value = part[0, which].astype(F32)
        value = value + moving[1, which][1].astype(F32) + moving[-1, which][1].astype(F32)
        sums.append(value.astype(BF16))
    returned = lax.all_to_all(
        jnp.concatenate(sums, axis=0).reshape(experts, cap, width), "expert", 0, 0, tiled=True
    ).reshape(slots, width)
    (down_grad,) = call(
        functools.partial(down_kernel, width),
        (struct((hid, model), BF16),),
        (*chunks, hidden),
        2 * slots * model * hid,
    )
    own_moe = dot(pick, returned, FIRST).astype(BF16)
    moe = lax.all_to_all(
        jnp.broadcast_to(own_moe[None], (n, tokens, width)), "tensor", 0, 0, tiled=True
    )
    resid_grad, attn_grad = call(
        tail_kernel,
        (struct((own, model), BF16), struct((tokens, out_proj.shape[0]), BF16)),
        (moe, all_rows, all_norm, norm_gain[None], proj),
        2 * tokens * model * out_proj.shape[0],
        (pltpu.VMEM((tokens, model), F32),),
    )
    return (resid_grad[None], attn_grad[None], down_grad[None])


def solution(mesh):
    placed = (
        P("expert", "tensor", None),
        P("expert", "tensor", None),
        P(),
        P("expert", None, None),
        P("expert", None, None),
        P("expert", None, "tensor"),
        P("expert", None, "tensor"),
        P("expert", None, "tensor"),
        P("expert", None, "tensor"),
        P("expert", "tensor", None),
        P("tensor", "expert"),
    )
    return jax.shard_map(
        per_device,
        mesh=mesh,
        in_specs=placed,
        out_specs=(
            P("expert", "tensor", None),
            P("expert", None, "tensor"),
            P("expert", "tensor", None),
        ),
        check_vma=False,
    )
```

```python
import functools
import math

import jax
import jax.numpy as jnp
from jax import lax
from jax.experimental import pallas as pl
from jax.experimental.pallas import tpu as pltpu
from jax.sharding import PartitionSpec as P

F32 = jnp.float32
BF16 = jnp.bfloat16
LAST = (((1,), (1,)), ((), ()))
FIRST = (((0,), (0,)), ((), ()))
PLAIN = (((1,), (0,)), ((), ()))
VMEM_BYTES = 16 * 1024 * 1024
OFFSETS = (0, 1, -1, 2, -2, 3, -3, 4)


def dot(a, b, dims):
    return lax.dot_general(a, b, dims, preferred_element_type=F32)


def vmem_specs(count):
    return [pl.BlockSpec(memory_space=pltpu.VMEM)] * count


def call(kernel, out_shapes, args, flops, scratch=(), out_specs=None):
    moved = sum(math.prod(a.shape) * a.dtype.itemsize for a in (*args, *out_shapes))
    return pl.pallas_call(
        kernel,
        out_shape=list(out_shapes),
        in_specs=vmem_specs(len(args)),
        out_specs=out_specs or vmem_specs(len(out_shapes)),
        scratch_shapes=list(scratch),
        compiler_params=pltpu.CompilerParams(vmem_limit_bytes=VMEM_BYTES),
        cost_estimate=pl.CostEstimate(flops=flops, bytes_accessed=moved, transcendentals=0),
    )(*args)


def struct(shape, dtype):
    return jax.ShapeDtypeStruct(shape, dtype)


def slice_at(offset, width):
    n = lax.axis_size("tensor")
    index = lax.rem(lax.axis_index("tensor") + (offset + n), n)
    return pl.ds(pl.multiple_of(index * width, width), width)


def ready_kernel(
    gate_ref, up_ref, w_down, w_gate, w_up, slope_ref, act_ref, hidden_ref, down_ref, side_ref
):
    gate = gate_ref[...].astype(F32)
    upper = up_ref[...].astype(F32)
    sig = jax.nn.sigmoid(gate)
    act = gate * sig
    slope_ref[...] = upper * sig * (1.0 + gate * (1.0 - sig))
    act_ref[...] = act
    hidden_ref[...] = (act * upper).T.astype(BF16)
    hid = w_gate.shape[1]
    down_ref[...] = w_down[...].T
    side_ref[:hid, :] = w_gate[...].T
    side_ref[hid:, :] = w_up[...].T


def early_kernel(width, *refs):
    chunks = refs[:14]
    hidden, down_ref, total_ref, out = refs[14:]
    rows = chunks[0].shape[0]
    for half in range(2):
        total = None
        for k, offset in enumerate(OFFSETS[:7]):
            term = dot(chunks[2 * k + half][...], down_ref[slice_at(offset, width), :], PLAIN)
            total = term if total is None else total + term
        total_ref[pl.ds(half * rows, rows), :] = total
    for k, offset in enumerate(OFFSETS[:7]):
        down = dot(hidden[:, :rows], chunks[2 * k][...], PLAIN)
        down = down + dot(hidden[:, rows:], chunks[2 * k + 1][...], PLAIN)
        out[:, slice_at(offset, width)] = down.astype(BF16)


def late_kernel(width, *refs):
    chunks, (hidden, total_ref, slope_ref, act_ref, down_ref, side_ref) = refs[:2], refs[2:8]
    part_hbm, out, grads_ref, part_ref, sems = refs[8:]
    rows = chunks[0].shape[0]
    hid = slope_ref.shape[1]
    cols = slice_at(OFFSETS[7], width)
    for half in range(2):
        here = pl.ds(half * rows, rows)
        total = total_ref[here, :] + dot(chunks[half][...], down_ref[cols, :], PLAIN)
        grads_ref[here, :hid] = (total * slope_ref[here, :]).astype(BF16)
        grads_ref[here, hid:] = (total * act_ref[here, :]).astype(BF16)
    copies = []
    for j in range(part_ref.shape[0]):
        for half in range(2):
            here = pl.ds(half * rows, rows)
            part = dot(grads_ref[here, :], side_ref[:, pl.ds(j * width, width)], PLAIN)
            part_ref[j, here, :] = part.astype(BF16)
        copies.append(pltpu.make_async_copy(part_ref.at[j], part_hbm.at[j], sems.at[j]))
        copies[-1].start()
    down = dot(hidden[:, :rows], chunks[0][...], PLAIN)
    down = down + dot(hidden[:, rows:], chunks[1][...], PLAIN)
    out[...] = down.astype(BF16)
    for copy in copies:
        copy.wait()


def token_kernel(pick_ref, slot_ref, out_ref):
    total = dot(pick_ref[...], slot_ref[...], FIRST).astype(BF16)
    for j in range(out_ref.shape[0]):
        out_ref[j] = total


def tail_kernel(moe_ref, rows_ref, norm_ref, gain_ref, proj_ref, resid_ref, attn_ref, held):
    n, _, width = moe_ref.shape
    model = n * width
    norm_in = norm_ref[...].astype(F32)
    inv = lax.rsqrt(jnp.sum(norm_in * norm_in, axis=-1, keepdims=True) / model + 1e-06)
    moe = jnp.concatenate([moe_ref[j] for j in range(n)], axis=1).astype(F32)
    scaled = gain_ref[...] * moe
    along = jnp.sum(scaled * norm_in, axis=-1, keepdims=True)
    resid = rows_ref[...].astype(F32) + inv * scaled - inv * inv * inv / model * norm_in * along
    held[...] = resid
    attn_ref[...] = dot(resid.astype(BF16), proj_ref[...], PLAIN).astype(BF16)
    own = resid_ref.shape[0]
    index = lax.axis_index("tensor")
    pair = held[pl.ds(pl.multiple_of(index // 2 * 2 * own, 2 * own), 2 * own), :]
    resid_ref[...] = jnp.where(lax.rem(index, 2) == 0, pair[:own], pair[own:]).astype(BF16)


def shift(x, step):
    n = lax.axis_size("tensor")
    return lax.ppermute(x, "tensor", [(i, (i + step) % n) for i in range(n)])


def per_device(
    out_grad,
    norm_input,
    norm_gain,
    routes,
    route_weight,
    gate_saved,
    up_saved,
    w_gate,
    w_up,
    w_down,
    out_proj,
):
    experts = lax.axis_size("expert")
    n = lax.axis_size("tensor")
    tokens, top = routes.shape[1:]
    slots = gate_saved.shape[1]
    cap = slots // experts
    hid = gate_saved.shape[2]
    model = out_grad.shape[2]
    width = model // n
    total = tokens * top
    half = slots // 2

    ids = routes[0].reshape(total)
    number = jnp.arange(total, dtype=jnp.int32)
    same = (ids[:, None] == ids[None, :]) & (number[None, :] < number[:, None])
    rank = jnp.sum(same.astype(jnp.int32), axis=1)
    position = ids * cap + rank
    named = position[None, :] == jnp.arange(slots, dtype=jnp.int32)[:, None]
    slot_weight = jnp.sum(
        jnp.where(named, route_weight[0].reshape(1, total), 0.0), axis=1, keepdims=True
    )
    of_token = (
        number[:, None] // top == jnp.arange(tokens, dtype=jnp.int32)[None, :]
    ).astype(BF16)
    pick = dot(named.astype(BF16), of_token, PLAIN).astype(BF16)

    own_rows = lax.all_to_all(out_grad[0], "tensor", 1, 0, tiled=True)
    scaled = (slot_weight * dot(pick, own_rows, PLAIN)).astype(BF16)
    own_slots = lax.all_to_all(
        scaled.reshape(experts, cap, width), "expert", 0, 0, tiled=True
    ).reshape(slots, width)

    own = out_grad.shape[1]
    both = jnp.concatenate([out_grad[0], norm_input[0]] * 2, axis=0)
    proj = lax.all_gather(out_proj.T, "expert", axis=0, tiled=True)
    wide = struct((slots, hid), F32)
    prepared = call(
        ready_kernel,
        (
            wide,
            wide,
            struct((hid, slots), BF16),
            struct((model, hid), BF16),
            struct((2 * hid, model), BF16),
        ),
        (gate_saved[0], up_saved[0], w_down[0], w_gate[0], w_up[0]),
        0,
    )
    own_slots, prepared, both = lax.optimization_barrier((own_slots, prepared, both))
    slope, act, hidden, down_t, side_t = prepared
    held = {(0, 0): own_slots[:half], (0, 1): own_slots[half:]}
    for step in range(1, 5):
        held[step, 0] = shift(held[step - 1, 0], 1)
        held[-step, 1] = shift(held[1 - step, 1], -1)
        if step < 4:
            held[step, 1] = shift(held[step - 1, 1], 1)
            held[-step, 0] = shift(held[1 - step, 0], -1)
    chunks = []
    for offset in OFFSETS:
        for which in range(2):
            key = -offset if offset != 4 else (4 if which == 0 else -4)
            chunks.append(held[key, which])

    total, down_grad = call(
        functools.partial(early_kernel, width),
        (struct((slots, hid), F32), struct((hid, model), BF16)),
        (*chunks[:14], hidden, down_t),
        4 * slots * model * hid,
    )
    part, last_down = call(
        functools.partial(late_kernel, width),
        (pltpu.HBM((n, slots, width), BF16), struct((hid, width), BF16)),
        (*chunks[14:], hidden, total, slope, act, down_t, side_t),
        4 * slots * model * hid,
        (
            pltpu.VMEM((slots, 2 * hid), BF16),
            pltpu.VMEM((n, slots, width), BF16),
            pltpu.SemaphoreType.DMA((n,)),
        ),
        [pl.BlockSpec(memory_space=pltpu.HBM), *vmem_specs(1)],
    )
    part, proj = lax.optimization_barrier((part, proj))
    sums = lax.psum_scatter(
        part.reshape(n * slots, width), "tensor", scatter_dimension=0, tiled=True
    )
    last = lax.rem(lax.axis_index("tensor") + OFFSETS[7], n) * width
    down_grad = lax.dynamic_update_slice(down_grad, last_down, (0, last))
    sums, both, down_grad = lax.optimization_barrier((sums, both, down_grad))
    every = lax.all_gather(both, "tensor", axis=0)
    all_rows = every[:, :own].reshape(tokens, model)
    all_norm = every[:, own : 2 * own].reshape(tokens, model)
    returned = lax.all_to_all(
        sums.reshape(experts, cap, width), "expert", 0, 0, tiled=True
    ).reshape(slots, width)
    (own_moe,) = call(
        token_kernel,
        (struct((n, tokens, width), BF16),),
        (pick, returned),
        2 * tokens * slots * width,
    )
    moe = lax.all_to_all(own_moe, "tensor", 0, 0, tiled=True)
    resid_grad, attn_grad = call(
        tail_kernel,
        (struct((own, model), BF16), struct((tokens, out_proj.shape[0]), BF16)),
        (moe, all_rows, all_norm, norm_gain[None], proj),
        2 * tokens * model * out_proj.shape[0],
        (pltpu.VMEM((tokens, model), F32),),
    )
    return (resid_grad[None], attn_grad[None], down_grad[None])


def solution(mesh):
    placed = (
        P("expert", "tensor", None),
        P("expert", "tensor", None),
        P(),
        P("expert", None, None),
        P("expert", None, None),
        P("expert", None, "tensor"),
        P("expert", None, "tensor"),
        P("expert", None, "tensor"),
        P("expert", None, "tensor"),
        P("expert", "tensor", None),
        P("tensor", "expert"),
    )
    return jax.shard_map(
        per_device,
        mesh=mesh,
        in_specs=placed,
        out_specs=(
            P("expert", "tensor", None),
            P("expert", None, "tensor"),
            P("expert", "tensor", None),
        ),
        check_vma=False,
    )
```

```python
import functools
import math

import jax
import jax.numpy as jnp
from jax import lax
from jax.experimental import pallas as pl
from jax.experimental.pallas import tpu as pltpu
from jax.sharding import PartitionSpec as P

F32 = jnp.float32
BF16 = jnp.bfloat16
LAST = (((1,), (1,)), ((), ()))
FIRST = (((0,), (0,)), ((), ()))
PLAIN = (((1,), (0,)), ((), ()))
VMEM_BYTES = 16 * 1024 * 1024
OFFSETS = (0, 1, -1, 2, -2, 3, -3, 4)


def dot(a, b, dims):
    return lax.dot_general(a, b, dims, preferred_element_type=F32)


def vmem_specs(count):
    return [pl.BlockSpec(memory_space=pltpu.VMEM)] * count


def call(kernel, out_shapes, args, flops, scratch=(), out_specs=None, in_specs=None, limit=VMEM_BYTES):
    moved = sum(math.prod(a.shape) * a.dtype.itemsize for a in (*args, *out_shapes))
    return pl.pallas_call(
        kernel,
        out_shape=list(out_shapes),
        in_specs=in_specs or vmem_specs(len(args)),
        out_specs=out_specs or vmem_specs(len(out_shapes)),
        scratch_shapes=list(scratch),
        compiler_params=pltpu.CompilerParams(vmem_limit_bytes=limit),
        cost_estimate=pl.CostEstimate(flops=flops, bytes_accessed=moved, transcendentals=0),
    )(*args)


def struct(shape, dtype):
    return jax.ShapeDtypeStruct(shape, dtype)


def slice_at(offset, width):
    n = lax.axis_size("tensor")
    index = lax.rem(lax.axis_index("tensor") + (offset + n), n)
    return pl.ds(pl.multiple_of(index * width, width), width)


def ready_kernel(
    gate_ref, up_ref, w_down, w_gate, w_up, slope_ref, act_ref, hidden_ref, down_ref, side_ref
):
    gate = gate_ref[...].astype(F32)
    upper = up_ref[...].astype(F32)
    sig = jax.nn.sigmoid(gate)
    act = gate * sig
    slope_ref[...] = upper * sig * (1.0 + gate * (1.0 - sig))
    act_ref[...] = act
    hidden_ref[...] = (act * upper).T.astype(BF16)
    hid = w_gate.shape[1]
    down_ref[...] = w_down[...].T
    side_ref[:hid, :] = w_gate[...].T
    side_ref[hid:, :] = w_up[...].T


def early_kernel(width, *refs):
    chunks = refs[:14]
    hidden, down_ref, total_ref, out = refs[14:]
    rows = chunks[0].shape[0]
    for half in range(2):
        total = None
        for k, offset in enumerate(OFFSETS[:7]):
            term = dot(chunks[2 * k + half][...], down_ref[slice_at(offset, width), :], PLAIN)
            total = term if total is None else total + term
        total_ref[pl.ds(half * rows, rows), :] = total
    for k, offset in enumerate(OFFSETS[:7]):
        down = dot(hidden[:, :rows], chunks[2 * k][...], PLAIN)
        down = down + dot(hidden[:, rows:], chunks[2 * k + 1][...], PLAIN)
        out[:, slice_at(offset, width)] = down.astype(BF16)


def late_kernel(width, *refs):
    chunks, (hidden, total_ref, slope_ref, act_ref, down_ref, side_ref) = refs[:2], refs[2:8]
    part_hbm, out_hbm, grads_ref, part_ref, down_part, sems = refs[8:]
    rows = chunks[0].shape[0]
    hid = slope_ref.shape[1]
    cols = slice_at(OFFSETS[7], width)
    for half in range(2):
        here = pl.ds(half * rows, rows)
        total = total_ref[here, :] + dot(chunks[half][...], down_ref[cols, :], PLAIN)
        grads_ref[here, :hid] = (total * slope_ref[here, :]).astype(BF16)
        grads_ref[here, hid:] = (total * act_ref[here, :]).astype(BF16)
    copies = []
    for j in range(part_ref.shape[0]):
        for half in range(2):
            here = pl.ds(half * rows, rows)
            part = dot(grads_ref[here, :], side_ref[:, pl.ds(j * width, width)], PLAIN)
            part_ref[j, here, :] = part.astype(BF16)
        copies.append(pltpu.make_async_copy(part_ref.at[j], part_hbm.at[j], sems.at[j]))
        copies[-1].start()
    down = dot(hidden[:, :rows], chunks[0][...], PLAIN)
    down = down + dot(hidden[:, rows:], chunks[1][...], PLAIN)
    down_part[...] = down.astype(BF16)
    copies.append(pltpu.make_async_copy(down_part, out_hbm, sems.at[len(copies)]))
    copies[-1].start()
    for copy in copies:
        copy.wait()


def token_kernel(pick_ref, slot_ref, out_ref):
    total = dot(pick_ref[...], slot_ref[...], FIRST).astype(BF16)
    for j in range(out_ref.shape[0]):
        out_ref[j] = total


def tail_kernel(
    moe_hbm,
    every_hbm,
    gain_hbm,
    proj_hbm,
    resid_ref,
    attn_ref,
    moe_ref,
    every_ref,
    gain_ref,
    proj_ref,
    rows_ref,
    norm_ref,
    sems,
):
    n, _, width = moe_ref.shape
    model = n * width
    own = resid_ref.shape[0]
    pieces = [pl.ds(j * width, width) for j in range(n)]
    pairs = [(every_hbm, every_ref), (moe_hbm, moe_ref), (gain_hbm, gain_ref)]
    pairs += [(proj_hbm.at[piece], proj_ref.at[piece]) for piece in pieces]
    copies = [pltpu.make_async_copy(a, b, sems.at[i]) for i, (a, b) in enumerate(pairs)]
    for copy in copies:
        copy.start()
    copies[0].wait()
    for j in range(n):
        both = every_ref[j].astype(F32)
        rows_ref[pl.ds(j * own, own), :] = both[:own]
        norm_ref[pl.ds(j * own, own), :] = both[own : 2 * own]
    norm_in = norm_ref[...]
    inv = lax.rsqrt(jnp.sum(norm_in * norm_in, axis=-1, keepdims=True) / model + 1e-06)
    copies[1].wait()
    copies[2].wait()
    moe = jnp.concatenate([moe_ref[j] for j in range(n)], axis=1).astype(F32)
    scaled = gain_ref[...] * moe
    along = jnp.sum(scaled * norm_in, axis=-1, keepdims=True)
    rows_ref[...] = (
        rows_ref[...] + inv * scaled - inv * inv * inv / model * norm_in * along
    )
    total = None
    for j, piece in enumerate(pieces):
        copies[3 + j].wait()
        term = dot(rows_ref[:, piece].astype(BF16), proj_ref[piece, :], PLAIN)
        total = term if total is None else total + term
    attn_ref[...] = total.astype(BF16)
    index = lax.axis_index("tensor")
    pair = rows_ref[pl.ds(pl.multiple_of(index // 2 * 2 * own, 2 * own), 2 * own), :]
    resid_ref[...] = jnp.where(lax.rem(index, 2) == 0, pair[:own], pair[own:]).astype(BF16)


def shift(x, step):
    n = lax.axis_size("tensor")
    return lax.ppermute(x, "tensor", [(i, (i + step) % n) for i in range(n)])


def per_device(
    out_grad,
    norm_input,
    norm_gain,
    routes,
    route_weight,
    gate_saved,
    up_saved,
    w_gate,
    w_up,
    w_down,
    out_proj,
):
    experts = lax.axis_size("expert")
    n = lax.axis_size("tensor")
    tokens, top = routes.shape[1:]
    slots = gate_saved.shape[1]
    cap = slots // experts
    hid = gate_saved.shape[2]
    model = out_grad.shape[2]
    width = model // n
    total = tokens * top
    half = slots // 2

    ids = routes[0].reshape(total)
    number = jnp.arange(total, dtype=jnp.int32)
    same = (ids[:, None] == ids[None, :]) & (number[None, :] < number[:, None])
    rank = jnp.sum(same.astype(jnp.int32), axis=1)
    position = ids * cap + rank
    named = position[None, :] == jnp.arange(slots, dtype=jnp.int32)[:, None]
    slot_weight = jnp.sum(
        jnp.where(named, route_weight[0].reshape(1, total), 0.0), axis=1, keepdims=True
    )
    of_token = (
        number[:, None] // top == jnp.arange(tokens, dtype=jnp.int32)[None, :]
    ).astype(BF16)
    pick = dot(named.astype(BF16), of_token, PLAIN).astype(BF16)

    own_rows = lax.all_to_all(out_grad[0], "tensor", 1, 0, tiled=True)
    scaled = (slot_weight * dot(pick, own_rows, PLAIN)).astype(BF16)
    own_slots = lax.all_to_all(
        scaled.reshape(experts, cap, width), "expert", 0, 0, tiled=True
    ).reshape(slots, width)

    own = out_grad.shape[1]
    both = jnp.concatenate([out_grad[0], norm_input[0]] * 2, axis=0)
    proj = lax.all_gather(out_proj.T, "expert", axis=0, tiled=True)
    wide = struct((slots, hid), F32)
    prepared = call(
        ready_kernel,
        (
            wide,
            wide,
            struct((hid, slots), BF16),
            struct((model, hid), BF16),
            struct((2 * hid, model), BF16),
        ),
        (gate_saved[0], up_saved[0], w_down[0], w_gate[0], w_up[0]),
        0,
    )
    own_slots, prepared, both = lax.optimization_barrier((own_slots, prepared, both))
    slope, act, hidden, down_t, side_t = prepared
    held = {(0, 0): own_slots[:half], (0, 1): own_slots[half:]}
    for step in range(1, 5):
        held[step, 0] = shift(held[step - 1, 0], 1)
        held[-step, 1] = shift(held[1 - step, 1], -1)
        if step < 4:
            held[step, 1] = shift(held[step - 1, 1], 1)
            held[-step, 0] = shift(held[1 - step, 0], -1)
    chunks = []
    for offset in OFFSETS:
        for which in range(2):
            key = -offset if offset != 4 else (4 if which == 0 else -4)
            chunks.append(held[key, which])

    total, down_grad = call(
        functools.partial(early_kernel, width),
        (struct((slots, hid), F32), struct((hid, model), BF16)),
        (*chunks[:14], hidden, down_t),
        4 * slots * model * hid,
    )
    part, last_down = call(
        functools.partial(late_kernel, width),
        (pltpu.HBM((n, slots, width), BF16), pltpu.HBM((hid, width), BF16)),
        (*chunks[14:], hidden, total, slope, act, down_t, side_t),
        4 * slots * model * hid,
        (
            pltpu.VMEM((slots, 2 * hid), BF16),
            pltpu.VMEM((n, slots, width), BF16),
            pltpu.VMEM((hid, width), BF16),
            pltpu.SemaphoreType.DMA((n + 1,)),
        ),
        [pl.BlockSpec(memory_space=pltpu.HBM)] * 2,
    )
    part, proj = lax.optimization_barrier((part, proj))
    sums = lax.psum_scatter(
        part.reshape(n * slots, width), "tensor", scatter_dimension=0, tiled=True
    )
    last = lax.rem(lax.axis_index("tensor") + OFFSETS[7], n) * width
    down_grad = lax.dynamic_update_slice(down_grad, last_down, (0, last))
    sums, both, down_grad = lax.optimization_barrier((sums, both, down_grad))
    every = lax.all_gather(both, "tensor", axis=0)
    returned = lax.all_to_all(
        sums.reshape(experts, cap, width), "expert", 0, 0, tiled=True
    ).reshape(slots, width)
    (own_moe,) = call(
        token_kernel,
        (struct((n, tokens, width), BF16),),
        (pick, returned),
        2 * tokens * slots * width,
    )
    moe = lax.all_to_all(own_moe, "tensor", 0, 0, tiled=True)
    resid_grad, attn_grad = call(
        tail_kernel,
        (struct((own, model), BF16), struct((tokens, out_proj.shape[0]), BF16)),
        (moe, every, norm_gain[None], proj),
        2 * tokens * model * out_proj.shape[0],
        (
            pltpu.VMEM(moe.shape, BF16),
            pltpu.VMEM(every.shape, BF16),
            pltpu.VMEM((1, model), F32),
            pltpu.VMEM(proj.shape, BF16),
            pltpu.VMEM((tokens, model), F32),
            pltpu.VMEM((tokens, model), F32),
            pltpu.SemaphoreType.DMA((3 + n,)),
        ),
        in_specs=[pl.BlockSpec(memory_space=pltpu.HBM)] * 4,
        limit=60 * 1024 * 1024,
    )
    return (resid_grad[None], attn_grad[None], down_grad[None])


def solution(mesh):
    placed = (
        P("expert", "tensor", None),
        P("expert", "tensor", None),
        P(),
        P("expert", None, None),
        P("expert", None, None),
        P("expert", None, "tensor"),
        P("expert", None, "tensor"),
        P("expert", None, "tensor"),
        P("expert", None, "tensor"),
        P("expert", "tensor", None),
        P("tensor", "expert"),
    )
    return jax.shard_map(
        per_device,
        mesh=mesh,
        in_specs=placed,
        out_specs=(
            P("expert", "tensor", None),
            P("expert", None, "tensor"),
            P("expert", "tensor", None),
        ),
        check_vma=False,
    )
```
